512 devices in a mesh: node: 32 (over y, z_hi, core), local: 16 (over z_lo, x).
Axes of the slice: x: 4, y: 8, z: 8 (z_hi: 2, z_lo: 4; z = z_hi * 4 + z_lo), core: 2. Of those that a mesh axis runs over, the one named last changes fastest.
Arguments:
- tokens: bfloat16 [2048, 4096], P('local', 'node'), may hold values from -6 to 6
- cotangent: bfloat16 [2048, 4096], P('local', 'node'), may hold values from -0.1875 to 0.1875
- gain: bfloat16 [1, 4096], P(None, 'node'), may hold values from 0.099609375 to 1.8984375
- up_q: bfloat16 [4096, 14336], P('local', 'node'), may hold values from -4 to 4
- up_scale: bfloat16 [32, 14336], P('local', 'node'), may hold values from 0.0078125 to 0.0390625
- down_q: bfloat16 [14336, 4096], P('node', 'local'), may hold values from -4 to 4
- down_scale: bfloat16 [14336, 32], P('node', 'local'), may hold values from 0.005004883 to 0.025024414
Outputs:
- states: bfloat16 [2048, 4096], P('local', 'node')
- grad_down: bfloat16 [14336, 4096], P('node', 'local')
The draws below stay inside these ranges and needn't reach their ends.
All inputs are finite; a program needn't handle non-finite values.
Results may differ from the reference program's by a relative error of at most 0.035.
Values may be sent and summed in bfloat16 or wider, within the bound.
A program may use at most 64 MiB of HBM per device.

```python
import math
import jax
import jax.numpy as jnp
from jax import lax

BLOCK = 128
D = 4096
FF = 14336
LOOPS = 2
TOK_DEV = 128
TOKENS = 2048
N_NODE = 32
N_LOCAL = 16


def raised(values, own_key, source, target, shards_of, factor):
    def block_of(dim):
        return (jnp.arange(values.shape[dim]) // (values.shape[dim] // shards_of)).reshape((-1,) + (1,) * (values.ndim - 1 - dim))

    one_side = jax.random.permutation(own_key, shards_of)[block_of(target)]
    second = (block_of(target) + shards_of // 2) % shards_of
    return jnp.where((block_of(source) == one_side) | (block_of(source) == second), factor * values, values)


def block_scale(rng, extent, cuts, low, top_value):
    level = 1.0
    for position, blocks in cuts:
        steps = jax.random.uniform(jax.random.fold_in(jax.random.fold_in(rng, 6), position), (blocks,), jnp.float32, low / len(cuts), top_value / len(cuts))
        level = level * jnp.repeat(jnp.exp(steps), extent[position] // blocks).reshape((-1,) + (1,) * (len(extent) - 1 - position))
    return level


def centred(rng, dims, spread, reach, shards=(), dtype=jnp.bfloat16):
    level = block_scale(rng, dims, shards, -0.22, 0.18) if shards else 1.0
    result = jax.random.normal(rng, dims, jnp.float32) * spread * level
    return jnp.minimum(jnp.maximum(result, -reach), reach).astype(dtype)


def noise_with(own_key, dims, spread, most, pieces, heavy, kind=jnp.bfloat16):
    drawn = spread * jax.random.normal(own_key, dims, jnp.float32)
    if pieces:
        drawn = drawn * block_scale(own_key, dims, pieces, -0.22, 0.18)
    return jnp.clip(raised(drawn, jax.random.fold_in(own_key, 3), *heavy), -most, most).astype(kind)


def setup_inputs(seed: int = 0) -> dict:
    seeds = jax.random.split(jax.random.key(seed), 8)
    return {
        "tokens": centred(seeds[0], (TOKENS, D), 1.0, 6.0, ((0, 16), (1, 32))),
        "cotangent": noise_with(seeds[1], (TOKENS, D), (1.0 / (TOKENS * LOOPS) ** 0.5), 0.1875, ((0, 16), (1, 32)), (0, 1, 32, 2.75)),
        "gain": jnp.clip(1.0 + 0.18 * jax.random.normal(seeds[2], (1, D), jnp.float32), 0.099609375, 1.8984375).astype(jnp.bfloat16),
        "up_q": centred(seeds[3], (D, FF), 1.0, 4.0, ((0, 16), (1, 32))),
        "up_scale": jnp.clip(jnp.exp(math.log(0.0390625) - 1.609438 * jax.random.uniform(seeds[4], (D // BLOCK, FF), jnp.float32) ** block_scale(seeds[4], (D // BLOCK, FF), ((0, 16), (1, 32)), -0.2, 0.2)), 0.0078125, 0.0390625).astype(jnp.bfloat16),
        "down_q": centred(seeds[5], (FF, D), 1.0, 4.0, ((0, 32), (1, 16))),
        "down_scale": jnp.clip(jnp.exp(math.log(0.025024414) - 1.609438 * jax.random.uniform(seeds[6], (FF, D // BLOCK), jnp.float32) ** block_scale(seeds[6], (FF, D // BLOCK), ((0, 32), (1, 16)), -0.2, 0.2)), 0.005004883, 0.025024414).astype(jnp.bfloat16),
    }


epsilon = 1e-05

def dequant_rows(quanta, scales):
    blocks = scales.shape[0]
    widened = quanta.astype(jnp.float32).reshape(blocks, quanta.shape[0] // blocks, quanta.shape[1])
    return (widened * scales.astype(jnp.float32)[:, None, :]).reshape(quanta.shape).astype(jnp.bfloat16)

def dequant_cols(quanta, scales):
    blocks = scales.shape[1]
    widened = quanta.astype(jnp.float32).reshape(quanta.shape[0], blocks, quanta.shape[1] // blocks)
    return (widened * scales.astype(jnp.float32)[:, :, None]).reshape(quanta.shape).astype(jnp.bfloat16)

def normalize(values, gains):
    widened = values.astype(jnp.float32)
    meansq = lax.optimization_barrier(jnp.mean(widened * widened, axis=-1, keepdims=True)) + epsilon
    factor = lax.rsqrt(meansq)
    return ((widened * factor * gains).astype(jnp.bfloat16), factor)

def norm_backward(values, factor, gains, upstream):
    widened = values.astype(jnp.float32)
    scaled = upstream * gains
    inner = lax.optimization_barrier(jnp.mean(scaled * widened, axis=-1, keepdims=True))
    return factor * scaled - widened * factor * factor * factor * inner

def silu_slope(pre):
    sigma = jax.nn.sigmoid(pre)
    return sigma * (1.0 + pre * (1.0 - sigma))

def grouped_product(left, right, groups):
    width = left.shape[1] // groups
    left_blocks = left.reshape(left.shape[0], groups, width).transpose(1, 0, 2)
    right_blocks = right.reshape(groups, width, right.shape[1])

    def accumulate(total, pair):
        part = jnp.dot(pair[0], pair[1], preferred_element_type=jnp.float32)
        kept = lax.optimization_barrier(part.astype(jnp.bfloat16))
        return (total + kept.astype(jnp.float32), None)
    start = jnp.zeros((left.shape[0], right.shape[1]), jnp.float32)
    total, _ = lax.scan(accumulate, start, (left_blocks, right_blocks))
    return total

def reference(tokens, cotangent, gain, up_q, up_scale, down_q, down_scale):
    up_weight = dequant_rows(up_q, up_scale)
    down_weight = dequant_cols(down_q, down_scale)
    gains = gain.astype(jnp.float32)
    values = tokens
    saved = []
    for loop_index in range(LOOPS):
        normed, factor = normalize(values, gains)
        pre = jnp.dot(normed, up_weight, preferred_element_type=jnp.float32)
        hidden = jax.nn.silu(pre).astype(jnp.bfloat16)
        update = grouped_product(hidden, down_weight, N_NODE)
        saved.append((values, factor, pre, hidden))
        values = (values.astype(jnp.float32) + update).astype(jnp.bfloat16)
    carried = cotangent
    activations = []
    gradients = []
    for loop_index in reversed(range(LOOPS)):
        before, factor, pre, hidden = saved[loop_index]
        activations.append(hidden)
        gradients.append(carried)
        if loop_index > 0:
            slope = jnp.dot(carried, down_weight.T, preferred_element_type=jnp.float32)
            pre_grad = (slope * silu_slope(pre)).astype(jnp.bfloat16)
            normed_grad = grouped_product(pre_grad, up_weight.T, N_NODE)
            carried = (carried.astype(jnp.float32) + norm_backward(before, factor, gains, normed_grad)).astype(jnp.bfloat16)
    stacked_acts = jnp.stack(activations).reshape(LOOPS, N_LOCAL, TOK_DEV, FF)
    stacked_acts = stacked_acts.transpose(1, 0, 2, 3).reshape(N_LOCAL, LOOPS * TOK_DEV, FF)
    stacked_grads = jnp.stack(gradients).reshape(LOOPS, N_LOCAL, TOK_DEV, D)
    stacked_grads = stacked_grads.transpose(1, 0, 2, 3).reshape(N_LOCAL, LOOPS * TOK_DEV, D)

    def add_group(total, pair):
        part = lax.dot_general(pair[0], pair[1], (((0,), (0,)), ((), ())), preferred_element_type=jnp.float32)
        kept = lax.optimization_barrier(part.astype(jnp.bfloat16))
        return (total + kept.astype(jnp.float32), None)
    grad_total, _ = lax.scan(add_group, jnp.zeros((FF, D), jnp.float32), (stacked_acts, stacked_grads))
    return (values, grad_total.astype(jnp.bfloat16))
```

```python
import jax
import jax.numpy as jnp
from jax import lax
from jax.experimental import pallas as pl
from jax.experimental.pallas import tpu as pltpu
from jax.sharding import PartitionSpec as P

MESH = pl.DeviceIdType.MESH
BF = jnp.bfloat16
F32 = jnp.float32
EPS = 1e-05
NT = (((1,), (1,)), ((), ()))
NN = (((1,), (0,)), ((), ()))


def dequant_rows(quanta, scales):
    blocks = scales.shape[0]
    widened = quanta.astype(F32).reshape(blocks, quanta.shape[0] // blocks, quanta.shape[1])
    return (widened * scales.astype(F32)[:, None, :]).reshape(quanta.shape).astype(BF)


def dequant_cols(quanta, scales):
    blocks = scales.shape[1]
    widened = quanta.astype(F32).reshape(quanta.shape[0], blocks, quanta.shape[1] // blocks)
    return (widened * scales.astype(F32)[:, :, None]).reshape(quanta.shape).astype(BF)


def peer(j):
    far = j // 2 + 1
    return far + (j % 2) * (8 - 2 * far)


def flip(a, i):
    return ((a // 2 + i // 2) % 2) * 2 + (a % 2 + i % 2) % 2


class Sems:
    def __init__(self):
        self.used = 0

    def take(self, count):
        base = self.used
        self.used += count
        return base


N_SEMS = 276


def kernel(
    up_in, dn_in, tok_in, cot_in, states_out, grad_out,
    up, dn, x0, x1, cot, cott, g1t, nb, h1t, h2t, hid, hf, pre, slope, gacc, fac, gp, tot,
    po1, ps1, r11, r21, r31, t31,
    pog, psg, r1g, r2g, r3g, t3g,
    po2, ps2, r12, r22, r32, t32,
    ss, rs,
):
    n = lax.axis_index("node")
    l = lax.axis_index("local")
    y, zh, c = n // 4, (n // 2) % 2, n % 2
    zl, x = l // 4, l % 4
    sems = Sems()

    def node_of(y_, zh_, c_):
        return (y_ * 2 + zh_) * 2 + c_

    sib = (node_of(y, zh, 1 - c), l)
    zhp = (node_of(y, 1 - zh, c), l)
    own_m = node_of(y, 1 - zh, c)

    def ydev(k):
        return (node_of((y + k) % 8, zh, c), l)

    def xdev(d):
        return (n, zl * 4 + (x + d + 4) % 4)

    def zdev(i):
        return (n, flip(zl, i) * 4 + x)

    part_n, part_l = l * 2 + c, n // 2
    moved = part_l != l
    part = (part_n, part_l)

    def rc(src, dst, sem, dev):
        return pltpu.make_async_remote_copy(
            src_ref=src, dst_ref=dst, send_sem=ss.at[sem], recv_sem=rs.at[sem],
            device_id=dev, device_id_type=MESH,
        )

    def loop(count, body):
        def step(j, carry):
            body(j)
            return carry
        lax.fori_loop(0, count, step, 0)

    class NodeGather:
        def __init__(self, buf):
            self.buf, self.base = buf, sems.take(31)

        def copy(self, slot, sem, dev):
            return rc(self.buf.at[slot], self.buf.at[slot], self.base + sem, dev)

        def own_y(self, j):
            return self.copy(n, 2 + j, ydev(peer(j)))

        def other_y(self, j):
            return self.copy(own_m, 9 + j, ydev(peer(j)))

        def from_y(self, j, zh_):
            return node_of((y - peer(j) + 8) % 8, zh_, c)

        def fwd_own(self, j):
            return self.copy(self.from_y(j, zh), 17 + j, sib)

        def fwd_other(self, j):
            return self.copy(self.from_y(j, 1 - zh), 24 + j, sib)

        def start(self):
            self.copy(n, 1, zhp).start()
            self.copy(n, 0, sib).start()
            loop(7, lambda j: self.own_y(j).start())

        def mid(self):
            self.copy(n, 1, zhp).wait_recv()
            loop(7, lambda j: self.other_y(j).start())
            self.copy(own_m, 16, sib).start()

        def forward(self):
            def first(j):
                self.own_y(j).wait_recv()
                self.fwd_own(j).start()

            def second(j):
                self.other_y(j).wait_recv()
                self.fwd_other(j).start()

            loop(7, first)
            loop(7, second)

        def end(self):
            self.copy(n, 0, sib).wait_recv()
            self.copy(own_m, 16, sib).wait_recv()
            loop(7, lambda j: self.fwd_own(j).wait_recv())
            loop(7, lambda j: self.fwd_other(j).wait_recv())

        def drain(self):
            self.copy(n, 0, sib).wait_send()
            self.copy(n, 1, zhp).wait_send()
            self.copy(own_m, 16, sib).wait_send()

            def sent(j):
                self.own_y(j).wait_send()
                self.other_y(j).wait_send()
                self.fwd_own(j).wait_send()
                self.fwd_other(j).wait_send()

            loop(7, sent)

    class LocalGather:
        def __init__(self, buf):
            self.buf, self.base = buf, sems.take(19)
            self.half = buf.shape[1] // 2

        def slot(self, i, d):
            return flip(zl, i) * 4 + (x + d + 4) % 4

        def zc(self, i):
            return rc(self.buf.at[l], self.buf.at[l], self.base + i - 1, zdev(i))

        def fc(self, i, d):
            s = self.slot(i, 0)
            return rc(self.buf.at[s], self.buf.at[s], self.base + 3 + 4 * i + (d < 0), xdev(d))

        def relc(self, i, d):
            s = self.slot(i, -d)
            rows = pl.ds(0 if d > 0 else self.half, self.half)
            ref = self.buf.at[s, rows]
            return rc(ref, ref, self.base + 5 + 4 * i + (d < 0), xdev(d))

        def z(self, i):
            self.zc(i).start()

        def wait_z(self, i):
            self.zc(i).wait_recv()

        def full(self, i):
            self.fc(i, 1).start()
            self.fc(i, -1).start()

        def relay(self, i):
            self.fc(i, 1).wait_recv()
            self.relc(i, 1).start()
            self.fc(i, -1).wait_recv()
            self.relc(i, -1).start()

        def done(self, i):
            self.relc(i, 1).wait_recv()
            self.relc(i, -1).wait_recv()

        def drain(self):
            for i in range(1, 4):
                self.zc(i).wait_send()
            for i in range(4):
                for d in (1, -1):
                    self.fc(i, d).wait_send()
                    self.relc(i, d).wait_send()

    class NodeReduce:
        def __init__(self, po, ps, r1, r2, r3, t3):
            self.po, self.ps, self.r1, self.r2, self.r3, self.t3 = po, ps, r1, r2, r3, t3
            self.base = sems.take(13)

        def sib_copy(self, i):
            rows = pl.ds(flip(zl, i) * 4, 4)
            return rc(self.ps.at[rows], self.r1.at[rows], self.base + i, sib)

        def y_copy(self, j):
            to = (y + peer(j)) % 8
            return rc(self.po.at[pl.ds(to * 2, 2)], self.r2.at[y], self.base + 4 + j, ydev(peer(j)))

        def zh_copy(self):
            return rc(self.t3, self.r3, self.base + 11, zhp)

        def send(self, i):
            self.sib_copy(i).start()

        def combine(self, i):
            self.sib_copy(i).wait_recv()
            first = flip(zl, i) * 4

            def add(q):
                s = first + q
                self.po[s] = (self.po[s].astype(F32) + self.r1[s].astype(F32)).astype(BF)

            loop(4, add)

        def spread(self):
            loop(7, lambda j: self.y_copy(j).start())

        def total(self, zh_):
            def add(j, acc):
                return acc + self.r2[(y - peer(j) + 8) % 8, zh_].astype(F32)

            return lax.fori_loop(0, 7, add, self.po[y * 2 + zh_].astype(F32))

        def cross(self):
            loop(7, lambda j: self.y_copy(j).wait_recv())
            self.t3[...] = self.total(1 - zh).astype(BF)
            self.zh_copy().start()

        def finish(self):
            mine = self.total(zh)
            self.zh_copy().wait_recv()
            return mine + self.r3[...].astype(F32)

        def drain(self):
            for i in range(4):
                self.sib_copy(i).wait_send()
            loop(7, lambda j: self.y_copy(j).wait_send())
            self.zh_copy().wait_send()

    perm_base = sems.take(2)

    def perm_copy(src, dst, which):
        return rc(src, dst.at[part_n], perm_base + which, part)

    def perm_start(src, dst, which):
        @pl.when(moved)
        def _():
            perm_copy(src, dst, which).start()

        @pl.when(jnp.logical_not(moved))
        def _():
            dst[n] = src[...]

    def perm_wait(src, dst, which):
        @pl.when(moved)
        def _():
            perm_copy(src, dst, which).wait_recv()

    def perm_drain(src, dst, which):
        @pl.when(moved)
        def _():
            perm_copy(src, dst, which).wait_send()

    def rms_factor(buf):
        def add(j, acc):
            v = buf[j, 0:128, :].astype(F32)
            return acc + v * v

        sums = lax.fori_loop(0, 32, add, jnp.zeros((128, 128), F32))
        factor = lax.rsqrt(jnp.sum(sums, axis=1, keepdims=True) / 4096.0 + EPS)
        fac[...] = jnp.broadcast_to(factor, (128, 128))

    def gain_row(j):
        return x0[j, 128:144, :].astype(F32)[0:1, :]

    def normalize(buf):
        rms_factor(buf)

        def one(q):
            for h in range(2):
                j = q * 2 + h
                v = buf[j, 0:128, :].astype(F32) * fac[...] * gain_row(j)
                nb[q, :, h * 128:(h + 1) * 128] = v.astype(BF)

        loop(16, one)

    def up_chunk(q):
        pre[...] += lax.dot_general(nb[q], up[q], NT, preferred_element_type=F32)

    def pre_item(i):
        loop(4, lambda q: up_chunk(flip(zl, i) * 4 + q))

    def slope_chunk(q):
        rows = jnp.concatenate([cot[q * 2], cot[q * 2 + 1]], axis=1)
        slope[...] += lax.dot_general(rows, dn[q], NT, preferred_element_type=F32)

    def activate(transposed):
        v = pre[...]
        h = v * jax.nn.sigmoid(v)
        hid[...] = h.astype(BF)
        hf[:, 0:448] = h
        for b in range(4):
            rows = 128 if b < 3 else 64
            block = hf[:, b * 128:(b + 1) * 128].T
            transposed[l, b * 128:b * 128 + rows, :] = block[0:rows, :].astype(BF)

    def out_chunk(left, weight, q, red):
        res = lax.dot_general(left, weight[q], NN, preferred_element_type=F32).astype(BF)
        low, high = res[:, 0:128], res[:, 128:256]
        even = c == 0
        red.po[q, 0:128, :] = jnp.where(even, low, high)
        red.ps[q, 0:128, :] = jnp.where(even, high, low)

    def out_item(left, weight, i, red):
        loop(4, lambda q: out_chunk(left[...], weight, flip(zl, i) * 4 + q, red))
        red.send(i)

    ag_x0, ag_cot, ag_cott, ag_x1, ag_g1 = (NodeGather(b) for b in (x0, cot, cott, x1, g1t))
    lg_up, lg_dn, lg_h1, lg_h2 = (LocalGather(b) for b in (up, dn, h1t, h2t))
    rs_1 = NodeReduce(po1, ps1, r11, r21, r31, t31)
    rs_g = NodeReduce(pog, psg, r1g, r2g, r3g, t3g)
    rs_2 = NodeReduce(po2, ps2, r12, r22, r32, t32)
    assert sems.used <= N_SEMS, sems.used

    barrier = pltpu.get_barrier_semaphore()

    def greet(dev):
        pl.semaphore_signal(barrier, inc=1, device_id=dev, device_id_type=MESH)

    @pl.when(moved)
    def _():
        greet(part)

    greet(zhp)
    loop(7, lambda j: greet(ydev(peer(j))))
    for i in range(1, 4):
        greet(zdev(i))
    greet(xdev(1))
    greet(xdev(-1))
    greet(sib)

    up[l] = up_in[...]
    dn[l] = dn_in[...]
    x0[n] = tok_in[...]
    cot[n] = cot_in[...]
    hf[...] = jnp.zeros_like(hf)
    pre[...] = jnp.zeros_like(pre)
    slope[...] = jnp.zeros_like(slope)

    @pl.when(moved)
    def _():
        pl.semaphore_wait(barrier, 15)

    @pl.when(jnp.logical_not(moved))
    def _():
        pl.semaphore_wait(barrier, 14)

    ag_x0.start()
    lg_up.z(1)
    lg_up.full(0)
    lg_up.z(2)
    perm_start(cot_in, cott, 0)
    ag_x0.mid()
    lg_up.relay(0)
    lg_up.wait_z(1)
    lg_up.z(3)
    lg_up.full(1)
    lg_up.wait_z(2)
    lg_up.full(2)
    ag_x0.forward()
    ag_cot.start()
    ag_x0.end()
    normalize(x0)
    lg_up.relay(1)
    lg_up.done(0)
    pre_item(0)
    lg_up.wait_z(3)
    lg_up.full(3)
    lg_dn.z(1)
    lg_dn.z(2)
    ag_cot.mid()
    lg_up.relay(2)
    lg_up.done(1)
    pre_item(1)
    lg_up.relay(3)
    lg_dn.full(0)
    lg_up.done(2)
    pre_item(2)
    lg_dn.wait_z(1)
    lg_dn.z(3)
    lg_dn.full(1)
    lg_up.done(3)
    pre_item(3)
    activate(h1t)
    lg_dn.relay(0)
    lg_dn.wait_z(2)
    lg_dn.full(2)
    ag_cot.forward()
    ag_cot.end()
    perm_wait(cot_in, cott, 0)
    ag_cott.start()
    lg_dn.relay(1)
    lg_dn.done(0)
    out_item(hid, dn, 0, rs_1)
    lg_dn.wait_z(3)
    lg_dn.full(3)
    ag_cott.mid()
    lg_dn.relay(2)
    lg_dn.done(1)
    out_item(hid, dn, 1, rs_1)
    rs_1.combine(0)
    lg_dn.relay(3)
    lg_dn.done(2)
    out_item(hid, dn, 2, rs_1)
    rs_1.combine(1)
    ag_cott.forward()
    lg_dn.done(3)
    out_item(hid, dn, 3, rs_1)
    rs_1.combine(2)
    rs_1.combine(3)
    rs_1.spread()
    for i in range(1, 4):
        lg_h1.z(i)
    loop(16, slope_chunk)
    rs_1.cross()
    lg_h1.full(0)
    for i in range(1, 4):
        lg_h1.wait_z(i)
        lg_h1.full(i)
    ag_cott.end()
    x1[n] = (x0[n, 0:128, :].astype(F32) + rs_1.finish()).astype(BF)

    ag_x1.start()
    pre[...] = jnp.zeros_like(pre)
    ag_x1.mid()
    for i in range(4):
        lg_h1.relay(i)
    ag_x1.forward()
    ag_x1.end()
    normalize(x1)
    loop(16, up_chunk)
    activate(h2t)

    v = pre[...]
    sig = jax.nn.sigmoid(v)
    grad_pre = (slope[...] * (sig * (1.0 + v * (1.0 - sig)))).astype(BF)
    pulled = jnp.sum(grad_pre.astype(F32) * v, axis=1, keepdims=True)
    pulled = jnp.broadcast_to(pulled, (128, 128)).T[0:16, :].astype(BF)

    def put(j):
        pog[j, 128:144, :] = pulled
        psg[j, 128:144, :] = pulled

    loop(16, put)
    for i in range(4):
        loop(4, lambda q: out_chunk(grad_pre, up, flip(zl, i) * 4 + q, rs_g))
        rs_g.send(i)
    for i in range(4):
        rs_g.combine(i)
    rs_g.spread()
    for i in range(1, 4):
        lg_h2.z(i)
    lg_h2.full(0)
    for i in range(4):
        out_item(hid, dn, i, rs_2)
    for i in range(4):
        rs_2.combine(i)
    rs_g.cross()
    rs_2.spread()
    for i in range(1, 4):
        lg_h2.wait_z(i)
        lg_h2.full(i)
    tot[...] = rs_g.finish()
    inner = jnp.broadcast_to(tot[128:129, :], (128, 128)).T / 4096.0
    x1_own = x1[n].astype(F32)
    scaled = tot[0:128, :] * gain_row(n)
    factor = fac[...]
    gp[...] = (cot[n].astype(F32) + factor * scaled - x1_own * factor * factor * inner).astype(BF)
    perm_start(gp, g1t, 1)
    for i in range(4):
        lg_h2.relay(i)
        lg_h1.done(i)
    perm_wait(gp, g1t, 1)
    ag_g1.start()
    rs_2.cross()
    gacc[...] = jnp.zeros_like(gacc)
    for i in range(4):
        lg_h2.done(i)

    def grad_chunk(hidden, grads):
        def one(q):
            right = jnp.concatenate([grads[q * 2], grads[q * 2 + 1]], axis=1)
            gacc[...] += lax.dot_general(hidden[q], right, NN, preferred_element_type=F32)
        return one

    ag_g1.mid()
    loop(16, grad_chunk(h2t, cott))
    states_out[...] = (x1_own + rs_2.finish()).astype(BF)
    ag_g1.forward()
    ag_g1.end()
    loop(16, grad_chunk(h1t, g1t))
    grad_out[...] = gacc[...].astype(BF)

    for g in (ag_x0, ag_cot, ag_cott, ag_x1, ag_g1, lg_up, lg_dn, lg_h1, lg_h2, rs_1, rs_g, rs_2):
        g.drain()
    perm_drain(cot_in, cott, 0)
    perm_drain(gp, g1t, 1)


def per_device(tokens, cotangent, gain, up_q, up_scale, down_q, down_scale):
    up = dequant_rows(up_q, up_scale).T
    down = dequant_cols(down_q, down_scale)
    tok = jnp.concatenate([tokens, jnp.broadcast_to(gain, (16, 128))], axis=0)
    vmem = pl.BlockSpec(memory_space=pltpu.VMEM)

    def reduce_scratch(rows):
        wide = pltpu.VMEM((16, rows, 128), BF)
        one = pltpu.VMEM((rows, 128), BF)
        return [wide, wide, wide, pltpu.VMEM((8, 2, rows, 128), BF), one, one]

    full = pltpu.VMEM((16, 448, 256), BF)
    act = pltpu.VMEM((32, 128, 128), BF)
    hidden_all = pltpu.VMEM((16, 448, 128), BF)
    scratch = [
        full, full, pltpu.VMEM((32, 144, 128), BF), act, act, act, act,
        pltpu.VMEM((16, 128, 256), BF), hidden_all, hidden_all,
        pltpu.VMEM((128, 448), BF), pltpu.VMEM((128, 512), F32),
        pltpu.VMEM((128, 448), F32), pltpu.VMEM((128, 448), F32),
        pltpu.VMEM((448, 256), F32), pltpu.VMEM((128, 128), F32),
        pltpu.VMEM((128, 128), BF), pltpu.VMEM((144, 128), F32),
    ]
    scratch += reduce_scratch(128) + reduce_scratch(144) + reduce_scratch(128)
    scratch += [pltpu.SemaphoreType.DMA((N_SEMS,)), pltpu.SemaphoreType.DMA((N_SEMS,))]
    return pl.pallas_call(
        kernel,
        out_shape=(
            jax.ShapeDtypeStruct((128, 128), BF),
            jax.ShapeDtypeStruct((448, 256), BF),
        ),
        in_specs=[vmem] * 4,
        out_specs=(vmem, vmem),
        scratch_shapes=scratch,
        compiler_params=pltpu.CompilerParams(
            collective_id=0, has_side_effects=True, vmem_limit_bytes=48 << 20
        ),
        name="looped_block",
    )(up, down, tok, cotangent)


def solution(mesh):
    in_specs = (
        P("local", "node"),
        P("local", "node"),
        P(None, "node"),
        P("local", "node"),
        P("local", "node"),
        P("node", "local"),
        P("node", "local"),
    )
    out_specs = (P("local", "node"), P("node", "local"))
    return jax.shard_map(
        per_device, mesh=mesh, in_specs=in_specs, out_specs=out_specs, check_vma=False
    )
```

```python
import jax
import jax.numpy as jnp
from jax import lax
from jax.experimental import pallas as pl
from jax.experimental.pallas import tpu as pltpu
from jax.sharding import PartitionSpec as P

MESH = pl.DeviceIdType.MESH
BF = jnp.bfloat16
F32 = jnp.float32
EPS = 1e-05
NT = (((1,), (1,)), ((), ()))
NN = (((1,), (0,)), ((), ()))


def peer(j):
    far = j // 2 + 1
    return far + (j % 2) * (8 - 2 * far)


def flip(a, i):
    return ((a // 2 + i // 2) % 2) * 2 + (a % 2 + i % 2) % 2


class Sems:
    def __init__(self):
        self.used = 0

    def take(self, count):
        base = self.used
        self.used += count
        return base


N_SEND = 24
N_RECV = 152


def kernel(
    tok_in, cot_in, gain_in, up_q, up_s, dn_q, dn_s, states_out, grad_out,
    up, dn, x0, x1, cot, cott, g1t, nb, h1t, h2t, hid, hf, pre, slope, gacc, fac, gp, tot,
    po1, ps1, r11, r21, r31, t31,
    pog, psg, r1g, r2g, r3g, t3g,
    po2, ps2, r12, r22, r32, t32,
    ss, rs,
):
    n = lax.axis_index("node")
    l = lax.axis_index("local")
    y, zh, c = n // 4, (n // 2) % 2, n % 2
    zl, x = l // 4, l % 4
    sends, recvs = Sems(), Sems()

    def node_of(y_, zh_, c_):
        return (y_ * 2 + zh_) * 2 + c_

    sib = (node_of(y, zh, 1 - c), l)
    zhp = (node_of(y, 1 - zh, c), l)
    own_m = node_of(y, 1 - zh, c)

    def ydev(k):
        return (node_of((y + k) % 8, zh, c), l)

    def xdev(d):
        return (n, zl * 4 + (x + d + 4) % 4)

    def zdev(i):
        return (n, flip(zl, i) * 4 + x)

    moved = n // 2 != l

    def rc(src, dst, send, recv, dev):
        return pltpu.make_async_remote_copy(
            src_ref=src, dst_ref=dst, send_sem=ss.at[send], recv_sem=rs.at[recv],
            device_id=dev, device_id_type=MESH,
        )

    def loop(count, body, first=0, unroll=1):
        if count - first == 1:
            body(first)
            return

        def step(j, carry):
            body(j)
            return carry

        lax.fori_loop(first, count, step, 0, unroll=unroll)

    pending = {}
    departures = []

    def go(key, count, copy):
        assert key not in pending
        pending[key] = count, copy
        loop(count, lambda j: copy(j).start())

    def got(key):
        count, copy = pending.pop(key)
        loop(count, lambda j: copy(j).wait_recv())

    def departing(view):
        sem = sends.take(1)
        departures.append((view, sem))
        return sem

    def drain():
        assert not pending
        for view, sem in departures:
            rc(view, view, sem, 0, sib).wait_send()

    class NodeGather:
        def __init__(self, buf, base):
            self.buf, self.base = buf, base
            self.left = departing(buf.at[pl.ds(0, 31)])

        def copy(self, slot, sem, dev):
            return rc(self.buf.at[slot], self.buf.at[slot], self.left, self.base + sem, dev)

        def from_y(self, j, zh_):
            return node_of((y - peer(j) + 8) % 8, zh_, c)

        def start(self):
            go((self, "zh"), 1, lambda j: self.copy(n, 1, zhp))
            go((self, "own"), 7, lambda j: self.copy(n, 2 + j, ydev(peer(j))))
            go((self, "sib"), 1, lambda j: self.copy(n, 0, sib))

        def mid(self):
            got((self, "zh"))
            go((self, "other"), 7, lambda j: self.copy(own_m, 9 + j, ydev(peer(j))))
            go((self, "sib_zh"), 1, lambda j: self.copy(own_m, 16, sib))

        def pass_on(self, key, zh_, sem, use):
            count, came = pending.pop((self, key))

            def copy(j):
                return self.copy(self.from_y(j, zh_), sem + j, sib)

            def move(j):
                came(j).wait_recv()
                copy(j).start()

            def finish(j):
                copy(j).wait_recv()
                use(((y - peer(j) + 8) % 8) * 2 + zh_)

            def both(j):
                move(j)
                finish(j - 1)

            move(0)
            loop(count, both, first=1)
            finish(count - 1)

        def end(self, use=lambda q: None):
            got((self, "sib"))
            use(y * 2 + zh)
            got((self, "sib_zh"))
            use(y * 2 + 1 - zh)
            self.pass_on("own", zh, 17, use)
            self.pass_on("other", 1 - zh, 24, use)

    class SeededGather:
        def __init__(self, buf, base):
            self.buf, self.base, self.perm = buf, base, recvs.take(4)
            self.left = departing(buf.at[pl.ds(0, 28)])
            self.perm_left = sends.take(4)

        def seed(self, k):
            return node_of((y + 4 * (k // 2)) % 8, (zh + k % 2) % 2, c)

        def scatter_copy(self, src, k):
            to = node_of((l // 2 + 4 * (k // 2)) % 8, (l % 2 + k % 2) % 2, c)
            return rc(src, self.buf.at[l * 2 + c], self.perm_left + k, self.perm + k, (to, n // 2))

        def scatter(self, src):
            @pl.when(moved)
            def _():
                self.scatter_copy(src, 0).start()

            @pl.when(jnp.logical_not(moved))
            def _():
                self.buf[l * 2 + c] = src[...]

            for k in range(1, 4):
                self.scatter_copy(src, k).start()

        def seeded(self, src):
            @pl.when(moved)
            def _():
                self.scatter_copy(src, 0).wait_recv()

            for k in range(1, 4):
                self.scatter_copy(src, k).wait_recv()

        def scattered(self, src):
            @pl.when(moved)
            def _():
                self.scatter_copy(src, 0).wait_send()

            for k in range(1, 4):
                self.scatter_copy(src, k).wait_send()

        def copy(self, slot, sem, dev):
            return rc(self.buf.at[slot], self.buf.at[slot], self.left, self.base + sem, dev)

        def step(self, r, k):
            return (1, 7)[r] if r < 2 else 2 + 4 * (k % 2)

        def spread(self):
            for r in range(3):
                loop(4, lambda k: self.copy(self.seed(k), r * 4 + k, ydev(self.step(r, k))).start())
            loop(4, lambda k: self.copy(self.seed(k), 12 + k, sib).start())

        def arrival(self, r, k):
            from_y = (y - self.step(r, k) + 8) % 8
            return node_of((from_y + 4 * (k // 2)) % 8, (zh + k % 2) % 2, c)

        def end(self, use):
            def move(r, k):
                slot = self.arrival(r, k)
                self.copy(slot, r * 4 + k, sib).wait_recv()
                self.copy(slot, 16 + r * 4 + k, sib).start()

            def finish(r, k):
                slot = self.arrival(r, k)
                self.copy(slot, 16 + r * 4 + k, sib).wait_recv()
                use(slot // 2)

            def seeds(k):
                self.copy(self.seed(k), 12 + k, sib).wait_recv()
                use(self.seed(k) // 2)

            loop(4, seeds)
            for r in range(3):
                loop(4, lambda k: move(r, k))
                if r > 0:
                    loop(4, lambda k: finish(r - 1, k))
            loop(4, lambda k: finish(2, k))

    class LocalGather:
        def __init__(self, buf, base):
            self.buf, self.base = buf, base
            self.half = buf.shape[1] // 2
            self.left = departing(buf.at[pl.ds(0, 15)])

        def slot(self, i, d):
            return flip(zl, i) * 4 + (x + d + 4) % 4

        def z(self, i):
            go((self, "z", i), 1, lambda j: rc(self.buf.at[l], self.buf.at[l], self.left, self.base + i - 1, zdev(i)))

        def wait_z(self, i):
            got((self, "z", i))

        def full(self, i):
            s = self.buf.at[self.slot(i, 0)]
            for d in (1, -1):
                go((self, "x", i, d), 1, lambda j, d=d: rc(s, s, self.left, self.base + 3 + 2 * i + (d < 0), xdev(d)))

        def relay(self, i):
            for d in (1, -1):
                ref = self.buf.at[self.slot(i, -d), pl.ds(0 if d > 0 else self.half, self.half)]
                got((self, "x", i, d))
                rc(ref, ref, self.left, self.base + 11 + i, xdev(d)).start()

        def done(self, i):
            s = self.buf.at[self.slot(i, 2)]
            rc(s, s, self.left, self.base + 11 + i, xdev(1)).wait_recv()

    class NodeReduce:
        def __init__(self, po, ps, r1, r2, r3, t3):
            self.po, self.ps, self.r1, self.r2, self.r3, self.t3 = po, ps, r1, r2, r3, t3
            self.base = recvs.take(7)
            self.sib_left = departing(ps)
            self.left = departing(po.at[pl.ds(0, 15)])

        def send(self, i):
            rows = pl.ds(flip(zl, i) * 4, 4)
            go((self, "sib", i), 1, lambda j: rc(self.ps.at[rows], self.r1.at[rows], self.sib_left, self.base + i, sib))

        def combine(self, i):
            got((self, "sib", i))
            first = flip(zl, i) * 4

            def add(q):
                s = first + q
                self.po[s] = (self.po[s].astype(F32) + self.r1[s].astype(F32)).astype(BF)

            loop(4, add, unroll=True)

        def spread(self, kind, i):
            for q in range(2):
                to = flip(zl, i) * 2 + q
                src = self.po.at[to * 2 + (1 - zh if kind == 0 else zh)]

                @pl.when(to != y)
                def _():
                    rc(src, self.r2.at[kind, y], self.left, self.base + 4 + kind, (node_of(to, zh, c), l)).start()

        def arrive(self, kind):
            view = self.r2.at[kind, pl.ds(0, 7)]
            rc(view, view, self.left, self.base + 4 + kind, sib).wait_recv()

        def total(self, kind):
            def add(j, acc):
                return acc + self.r2[kind, (y - peer(j) + 8) % 8].astype(F32)

            return lax.fori_loop(0, 7, add, self.po[y * 2 + (1 - zh if kind == 0 else zh)].astype(F32), unroll=True)

        def cross(self):
            self.arrive(0)
            self.t3[...] = self.total(0).astype(BF)
            go((self, "zh"), 1, lambda j: rc(self.t3, self.r3, self.left, self.base + 6, zhp))

        def finish(self):
            mine = self.total(1)
            got((self, "zh"))
            return mine + self.r3[...].astype(F32)

    def factor_of(sums):
        return lax.rsqrt(jnp.sum(sums, axis=1, keepdims=True) / 4096.0 + EPS)

    def rms_factor(buf):
        def add(j, acc):
            v = buf[j, 0:128, :].astype(F32)
            return acc + v * v

        sums = lax.fori_loop(0, 32, add, jnp.zeros((128, 128), F32), unroll=4)
        fac[...] = jnp.broadcast_to(factor_of(sums), (128, 128))

    def gain_row(j):
        return x0[j, 128:144, :].astype(F32)[0:1, :]

    def normalize(buf):
        rms_factor(buf)

        def one(q):
            for h in range(2):
                j = q * 2 + h
                v = buf[j, 0:128, :].astype(F32) * fac[...] * gain_row(j)
                nb[q, :, h * 128:(h + 1) * 128] = v.astype(BF)

        loop(16, one, unroll=4)

    def up_chunk(q):
        pre[...] += lax.dot_general(nb[q], up[q], NT, preferred_element_type=F32)

    def pre_item(i):
        loop(4, lambda q: up_chunk(flip(zl, i) * 4 + q), unroll=True)

    def raw_chunk(q):
        halves = []
        for h in range(2):
            v = x1[q * 2 + h].astype(F32)
            fac[...] += v * v
            halves.append((v * gain_row(q * 2 + h)).astype(BF))
        pre[...] += lax.dot_general(jnp.concatenate(halves, axis=1), up[q], NT, preferred_element_type=F32)

    def slope_chunk(q):
        rows = jnp.concatenate([cot[q * 2], cot[q * 2 + 1]], axis=1)
        slope[...] += lax.dot_general(rows, dn[q], NT, preferred_element_type=F32)

    def activate(transposed):
        v = pre[...]
        h = v * jax.nn.sigmoid(v)
        hid[...] = h.astype(BF)
        hf[:, 0:448] = h
        for b in range(4):
            rows = 128 if b < 3 else 64
            block = hf[:, b * 128:(b + 1) * 128].T
            transposed[l, b * 128:b * 128 + rows, :] = block[0:rows, :].astype(BF)

    def out_chunk(left, weight, q, red):
        res = lax.dot_general(left, weight[q], NN, preferred_element_type=F32).astype(BF)
        low, high = res[:, 0:128], res[:, 128:256]
        even = c == 0
        red.po[q, 0:128, :] = jnp.where(even, low, high)
        red.ps[q, 0:128, :] = jnp.where(even, high, low)

    def out_item(left, weight, i, red):
        loop(4, lambda q: out_chunk(left[...], weight, flip(zl, i) * 4 + q, red), unroll=True)
        red.send(i)

    ag_a, ag_b, sg_a, lg_a, lg_b = (recvs.take(k) for k in (31, 31, 28, 15, 15))
    ag_x0, ag_cot, ag_x1 = NodeGather(x0, ag_a), NodeGather(cot, ag_b), NodeGather(x1, ag_a)
    sg_cot, sg_g1 = SeededGather(cott, sg_a), SeededGather(g1t, sg_a)
    lg_up, lg_dn = LocalGather(up, lg_a), LocalGather(dn, lg_b)
    lg_h1, lg_h2 = LocalGather(h1t, lg_a), LocalGather(h2t, lg_b)
    rs_1 = NodeReduce(po1, ps1, r11, r21, r31, t31)
    rs_g = NodeReduce(pog, psg, r1g, r2g, r3g, t3g)
    rs_2 = NodeReduce(po2, ps2, r12, r22, r32, t32)
    assert sends.used <= N_SEND and recvs.used <= N_RECV, (sends.used, recvs.used)

    barrier = pltpu.get_barrier_semaphore()

    def greet(dev):
        pl.semaphore_signal(barrier, inc=1, device_id=dev, device_id_type=MESH)

    for k in range(4):
        source = node_of((y + 4 * (k // 2)) % 8, (zh + k % 2) % 2, c) // 2
        if k == 0:
            @pl.when(moved)
            def _():
                greet((l * 2 + c, source))
        else:
            greet((l * 2 + c, source))

    greet(zhp)
    loop(7, lambda j: greet(ydev(peer(j))))
    for i in range(1, 4):
        greet(zdev(i))
    greet(xdev(1))
    greet(xdev(-1))
    greet(sib)

    hf[...] = jnp.zeros_like(hf)
    x0[n, 0:128, :] = tok_in[...]
    x0[n, 128:144, :] = jnp.broadcast_to(gain_in[...].astype(F32), (16, 128)).astype(BF)
    for a in range(2):
        hf[:, 0:448] = up_q[a * 128:(a + 1) * 128, :].astype(F32) * up_s[...].astype(F32)[a:a + 1, :]
        for b in range(4):
            rows = 128 if b < 3 else 64
            block = hf[:, b * 128:(b + 1) * 128].T
            up[l, b * 128:b * 128 + rows, a * 128:(a + 1) * 128] = block[0:rows, :].astype(BF)
        block = dn_q[:, a * 128:(a + 1) * 128].astype(F32) * dn_s[...].astype(F32)[:, a:a + 1]
        dn[l, :, a * 128:(a + 1) * 128] = block.astype(BF)
    cot[n] = cot_in[...]
    pre[...] = jnp.zeros_like(pre)
    slope[...] = jnp.zeros_like(slope)

    @pl.when(moved)
    def _():
        pl.semaphore_wait(barrier, 18)

    @pl.when(jnp.logical_not(moved))
    def _():
        pl.semaphore_wait(barrier, 17)

    lg_up.z(1)
    lg_up.full(0)
    ag_x0.start()
    lg_up.z(2)
    lg_dn.full(0)
    sg_cot.scatter(cot_in)
    ag_x0.mid()
    lg_up.relay(0)
    lg_up.wait_z(1)
    lg_up.full(1)
    lg_up.z(3)
    lg_dn.relay(0)
    lg_up.wait_z(2)
    lg_up.full(2)
    lg_dn.z(1)
    ag_x0.end()
    ag_cot.start()
    normalize(x0)
    lg_up.done(0)
    pre_item(0)
    lg_up.relay(1)
    lg_up.wait_z(3)
    lg_up.full(3)
    lg_dn.z(2)
    lg_up.relay(2)
    ag_cot.mid()
    lg_dn.wait_z(1)
    lg_dn.full(1)
    lg_dn.z(3)
    lg_up.done(1)
    pre_item(1)
    lg_up.relay(3)
    lg_dn.wait_z(2)
    lg_dn.full(2)
    lg_up.done(2)
    pre_item(2)
    lg_dn.relay(1)
    lg_dn.wait_z(3)
    lg_dn.full(3)
    lg_up.done(3)
    pre_item(3)
    activate(h1t)
    lg_dn.done(0)
    out_item(hid, dn, 0, rs_1)
    sg_cot.seeded(cot_in)
    sg_cot.spread()
    lg_dn.relay(2)
    rs_1.combine(0)
    rs_1.spread(0, 0)
    rs_1.spread(1, 0)
    lg_dn.done(1)
    out_item(hid, dn, 1, rs_1)
    lg_dn.relay(3)
    rs_1.combine(1)
    rs_1.spread(0, 1)
    rs_1.spread(1, 1)
    lg_dn.done(2)
    out_item(hid, dn, 2, rs_1)
    rs_1.combine(2)
    rs_1.spread(0, 2)
    rs_1.spread(1, 2)
    lg_dn.done(3)
    out_item(hid, dn, 3, rs_1)
    rs_1.combine(3)
    rs_1.spread(0, 3)
    rs_1.spread(1, 3)
    ag_cot.end(slope_chunk)
    rs_1.cross()
    sg_cot.end(lambda q: None)
    rs_1.arrive(1)
    x1[n] = (x0[n, 0:128, :].astype(F32) + rs_1.finish()).astype(BF)

    ag_x1.start()
    pre[...] = jnp.zeros_like(pre)
    fac[...] = jnp.zeros_like(fac)
    ag_x1.mid()
    for i in range(1, 4):
        lg_h1.z(i)
    lg_h1.full(0)
    ag_x1.end(raw_chunk)
    factor = factor_of(fac[...])
    fac[...] = jnp.broadcast_to(factor, (128, 128))
    pre[...] = pre[...] * factor
    activate(h2t)
    for i in range(1, 4):
        lg_h1.wait_z(i)
        lg_h1.full(i)
    for i in range(1, 4):
        lg_h2.z(i)

    v = pre[...]
    sig = jax.nn.sigmoid(v)
    grad_pre = (slope[...] * (sig * (1.0 + v * (1.0 - sig)))).astype(BF)
    pulled = jnp.sum(grad_pre.astype(F32) * v, axis=1, keepdims=True)
    pulled = jnp.broadcast_to(pulled, (128, 128)).T[0:16, :].astype(BF)

    def put(j):
        pog[j, 128:144, :] = pulled
        psg[j, 128:144, :] = pulled

    loop(16, put)
    for i in range(4):
        loop(4, lambda q: out_chunk(grad_pre, up, flip(zl, i) * 4 + q, rs_g), unroll=True)
        rs_g.send(i)
        if i > 0:
            rs_g.combine(i - 1)
            rs_g.spread(0, i - 1)
    rs_g.combine(3)
    rs_g.spread(0, 3)
    for i in range(4):
        rs_g.spread(1, i)
    for i in range(4):
        out_item(hid, dn, i, rs_2)
    for i in range(4):
        rs_2.combine(i)
    rs_g.cross()
    for i in range(4):
        lg_h1.relay(i)
    rs_g.arrive(1)
    for i in range(4):
        rs_2.spread(0, i)
    for i in range(4):
        rs_2.spread(1, i)
    tot[...] = rs_g.finish()
    inner = jnp.broadcast_to(tot[128:129, :], (128, 128)).T / 4096.0
    x1_own = x1[n].astype(F32)
    scaled = tot[0:128, :] * gain_row(n)
    factor = fac[...]
    gp[...] = (cot[n].astype(F32) + factor * scaled - x1_own * factor * factor * inner).astype(BF)
    sg_g1.scatter(gp)
    lg_h2.full(0)
    for i in range(1, 4):
        lg_h2.wait_z(i)
        lg_h2.full(i)
    for i in range(4):
        lg_h1.done(i)
    gacc[...] = jnp.zeros_like(gacc)
    rs_2.cross()
    sg_g1.seeded(gp)
    sg_g1.spread()
    rs_2.arrive(1)

    def grad_chunk(hidden, grads):
        def one(q):
            right = jnp.concatenate([grads[q * 2], grads[q * 2 + 1]], axis=1)
            gacc[...] += lax.dot_general(hidden[q], right, NN, preferred_element_type=F32)
        return one

    for i in range(4):
        lg_h2.relay(i)
    states_out[...] = (x1_own + rs_2.finish()).astype(BF)
    for i in range(4):
        lg_h2.done(i)
        loop(4, lambda q: grad_chunk(h2t, cott)(flip(zl, i) * 4 + q), unroll=True)
    last = grad_chunk(h1t, g1t)
    sg_g1.end(lambda q: None)
    loop(16, last, unroll=4)
    grad_out[...] = gacc[...].astype(BF)
    sg_cot.scattered(cot_in)
    sg_g1.scattered(gp)
    drain()


def per_device(tokens, cotangent, gain, up_q, up_scale, down_q, down_scale):
    vmem = pl.BlockSpec(memory_space=pltpu.VMEM)

    def reduce_scratch(rows):
        wide = pltpu.VMEM((16, rows, 128), BF)
        one = pltpu.VMEM((rows, 128), BF)
        return [wide, wide, wide, pltpu.VMEM((2, 8, rows, 128), BF), one, one]

    full = pltpu.VMEM((16, 448, 256), BF)
    act = pltpu.VMEM((32, 128, 128), BF)
    hidden_all = pltpu.VMEM((16, 448, 128), BF)
    scratch = [
        full, full, pltpu.VMEM((32, 144, 128), BF), act, act, act, act,
        pltpu.VMEM((16, 128, 256), BF), hidden_all, hidden_all,
        pltpu.VMEM((128, 448), BF), pltpu.VMEM((128, 512), F32),
        pltpu.VMEM((128, 448), F32), pltpu.VMEM((128, 448), F32),
        pltpu.VMEM((448, 256), F32), pltpu.VMEM((128, 128), F32),
        pltpu.VMEM((128, 128), BF), pltpu.VMEM((144, 128), F32),
    ]
    scratch += reduce_scratch(128) + reduce_scratch(144) + reduce_scratch(128)
    scratch += [pltpu.SemaphoreType.DMA((N_SEND,)), pltpu.SemaphoreType.DMA((N_RECV,))]
    return pl.pallas_call(
        kernel,
        out_shape=(
            jax.ShapeDtypeStruct((128, 128), BF),
            jax.ShapeDtypeStruct((448, 256), BF),
        ),
        in_specs=[vmem] * 7,
        out_specs=(vmem, vmem),
        scratch_shapes=scratch,
        compiler_params=pltpu.CompilerParams(
            collective_id=0, has_side_effects=True, vmem_limit_bytes=48 << 20
        ),
        name="looped_block",
    )(tokens, cotangent, gain, up_q, up_scale, down_q, down_scale)


def solution(mesh):
    in_specs = (
        P("local", "node"),
        P("local", "node"),
        P(None, "node"),
        P("local", "node"),
        P("local", "node"),
        P("node", "local"),
        P("node", "local"),
    )
    out_specs = (P("local", "node"), P("node", "local"))
    return jax.shard_map(
        per_device, mesh=mesh, in_specs=in_specs, out_specs=out_specs, check_vma=False
    )
```

```python
import jax
import jax.numpy as jnp
from jax import lax
from jax.experimental import pallas as pl
from jax.experimental.pallas import tpu as pltpu
from jax.sharding import PartitionSpec as P

MESH = pl.DeviceIdType.MESH
BF = jnp.bfloat16
F32 = jnp.float32
EPS = 1e-05
NT = (((1,), (1,)), ((), ()))
NN = (((1,), (0,)), ((), ()))


def peer(j):
    far = j // 2 + 1
    return far + (j % 2) * (8 - 2 * far)


def flip(a, i):
    return ((a // 2 + i // 2) % 2) * 2 + (a % 2 + i % 2) % 2


class Sems:
    def __init__(self):
        self.used = 0

    def take(self, count):
        base = self.used
        self.used += count
        return base


N_SEND = 24
N_RECV = 152


def kernel(
    tok_in, cot_in, gain_in, up_q, up_s, dn_q, dn_s, states_out, grad_out,
    up, dn, x0, x1, cot, cott, g1t, nb, h1t, h2t, hid, hf, pre, slope, gacc, fac, gp, tot,
    po1, ps1, r11, r21, r31, t31,
    pog, psg, r1g, r2g, r3g, t3g,
    po2, ps2, r12, r22, r32, t32,
    ss, rs,
):
    n = lax.axis_index("node")
    l = lax.axis_index("local")
    y, zh, c = n // 4, (n // 2) % 2, n % 2
    zl, x = l // 4, l % 4
    sends, recvs = Sems(), Sems()

    def node_of(y_, zh_, c_):
        return (y_ * 2 + zh_) * 2 + c_

    sib = (node_of(y, zh, 1 - c), l)
    zhp = (node_of(y, 1 - zh, c), l)
    own_m = node_of(y, 1 - zh, c)

    def ydev(k):
        return (node_of((y + k) % 8, zh, c), l)

    def xdev(d):
        return (n, zl * 4 + (x + d + 4) % 4)

    def zdev(i):
        return (n, flip(zl, i) * 4 + x)

    moved = n // 2 != l

    def rc(src, dst, send, recv, dev):
        return pltpu.make_async_remote_copy(
            src_ref=src, dst_ref=dst, send_sem=ss.at[send], recv_sem=rs.at[recv],
            device_id=dev, device_id_type=MESH,
        )

    def loop(count, body, first=0, unroll=1):
        if count - first == 1:
            body(first)
            return

        def step(j, carry):
            body(j)
            return carry

        lax.fori_loop(first, count, step, 0, unroll=unroll)

    pending = {}
    departures = []

    def go(key, count, copy):
        assert key not in pending
        pending[key] = count, copy
        loop(count, lambda j: copy(j).start())

    def got(key):
        count, copy = pending.pop(key)
        loop(count, lambda j: copy(j).wait_recv())

    def departing(view):
        sem = sends.take(1)
        departures.append((view, sem))
        return sem

    def drain():
        assert not pending
        for view, sem in departures:
            rc(view, view, sem, 0, sib).wait_send()

    class NodeGather:
        def __init__(self, buf, base):
            self.buf, self.base = buf, base
            self.left = departing(buf.at[pl.ds(0, 31)])

        def copy(self, slot, sem, dev):
            return rc(self.buf.at[slot], self.buf.at[slot], self.left, self.base + sem, dev)

        def from_y(self, j, zh_):
            return node_of((y - peer(j) + 8) % 8, zh_, c)

        def start(self):
            go((self, "zh"), 1, lambda j: self.copy(n, 1, zhp))
            go((self, "own"), 7, lambda j: self.copy(n, 2 + j, ydev(peer(j))))
            go((self, "sib"), 1, lambda j: self.copy(n, 0, sib))

        def mid(self):
            got((self, "zh"))
            go((self, "other"), 7, lambda j: self.copy(own_m, 9 + j, ydev(peer(j))))
            go((self, "sib_zh"), 1, lambda j: self.copy(own_m, 16, sib))

        def pass_on(self, key, zh_, sem, use):
            count, came = pending.pop((self, key))

            def copy(j):
                return self.copy(self.from_y(j, zh_), sem + j, sib)

            def move(j):
                came(j).wait_recv()
                copy(j).start()

            def finish(j):
                copy(j).wait_recv()
                use(((y - peer(j) + 8) % 8) * 2 + zh_)

            def both(j):
                move(j)
                finish(j - 1)

            move(0)
            loop(count, both, first=1)
            finish(count - 1)

        def end(self, use=lambda q: None):
            got((self, "sib"))
            use(y * 2 + zh)
            got((self, "sib_zh"))
            use(y * 2 + 1 - zh)
            self.pass_on("own", zh, 17, use)
            self.pass_on("other", 1 - zh, 24, use)

    class SeededGather:
        def __init__(self, buf, base):
            self.buf, self.base, self.perm = buf, base, recvs.take(4)
            self.left = departing(buf.at[pl.ds(0, 28)])
            self.perm_left = sends.take(4)

        def seed(self, k):
            return node_of((y + 4 * (k // 2)) % 8, (zh + k % 2) % 2, c)

        def scatter_copy(self, src, k):
            to = node_of((l // 2 + 4 * (k // 2)) % 8, (l % 2 + k % 2) % 2, c)
            return rc(src, self.buf.at[l * 2 + c], self.perm_left + k, self.perm + k, (to, n // 2))

        def scatter(self, src):
            @pl.when(moved)
            def _():
                self.scatter_copy(src, 0).start()

            @pl.when(jnp.logical_not(moved))
            def _():
                self.buf[l * 2 + c] = src[...]

            for k in range(1, 4):
                self.scatter_copy(src, k).start()

        def seeded(self, src):
            @pl.when(moved)
            def _():
                self.scatter_copy(src, 0).wait_recv()

            for k in range(1, 4):
                self.scatter_copy(src, k).wait_recv()

        def scattered(self, src):
            @pl.when(moved)
            def _():
                self.scatter_copy(src, 0).wait_send()

            for k in range(1, 4):
                self.scatter_copy(src, k).wait_send()

        def copy(self, slot, sem, dev):
            return rc(self.buf.at[slot], self.buf.at[slot], self.left, self.base + sem, dev)

        def step(self, r, k):
            return (1, 7)[r] if r < 2 else 2 + 4 * (k % 2)

        def spread(self):
            for r in range(3):
                loop(4, lambda k: self.copy(self.seed(k), r * 4 + k, ydev(self.step(r, k))).start())
            loop(4, lambda k: self.copy(self.seed(k), 12 + k, sib).start())

        def arrival(self, r, k):
            from_y = (y - self.step(r, k) + 8) % 8
            return node_of((from_y + 4 * (k // 2)) % 8, (zh + k % 2) % 2, c)

        def end(self, use, between=lambda: None):
            def move(r, k):
                slot = self.arrival(r, k)
                self.copy(slot, r * 4 + k, sib).wait_recv()
                self.copy(slot, 16 + r * 4 + k, sib).start()

            def finish(r, k):
                slot = self.arrival(r, k)
                self.copy(slot, 16 + r * 4 + k, sib).wait_recv()
                use(slot // 2)

            def seeds(k):
                self.copy(self.seed(k), 12 + k, sib).wait_recv()
                use(self.seed(k) // 2)

            loop(4, seeds)
            for r in range(3):
                if r == 2:
                    between()
                loop(4, lambda k: move(r, k))
                if r > 0:
                    loop(4, lambda k: finish(r - 1, k))
            loop(4, lambda k: finish(2, k))

    class LocalGather:
        def __init__(self, buf, base):
            self.buf, self.base = buf, base
            self.half = buf.shape[1] // 2
            self.left = departing(buf.at[pl.ds(0, 15)])

        def slot(self, i, d):
            return flip(zl, i) * 4 + (x + d + 4) % 4

        def z(self, i):
            go((self, "z", i), 1, lambda j: rc(self.buf.at[l], self.buf.at[l], self.left, self.base + i - 1, zdev(i)))

        def wait_z(self, i):
            got((self, "z", i))

        def full(self, i):
            s = self.buf.at[self.slot(i, 0)]
            for d in (1, -1):
                go((self, "x", i, d), 1, lambda j, d=d: rc(s, s, self.left, self.base + 3 + 2 * i + (d < 0), xdev(d)))

        def relay(self, i):
            for d in (1, -1):
                ref = self.buf.at[self.slot(i, -d), pl.ds(0 if d > 0 else self.half, self.half)]
                got((self, "x", i, d))
                rc(ref, ref, self.left, self.base + 11 + i, xdev(d)).start()

        def done(self, i):
            s = self.buf.at[self.slot(i, 2)]
            rc(s, s, self.left, self.base + 11 + i, xdev(1)).wait_recv()

    class NodeReduce:
        def __init__(self, po, ps, r1, r2, r3, t3):
            self.po, self.ps, self.r1, self.r2, self.r3, self.t3 = po, ps, r1, r2, r3, t3
            self.base = recvs.take(7)
            self.sib_left = departing(ps)
            self.left = departing(po.at[pl.ds(0, 15)])

        def send(self, i):
            rows = pl.ds(flip(zl, i) * 4, 4)
            go((self, "sib", i), 1, lambda j: rc(self.ps.at[rows], self.r1.at[rows], self.sib_left, self.base + i, sib))

        def combine(self, i):
            got((self, "sib", i))
            loop(4, lambda q: self.add_chunk(flip(zl, i) * 4 + q), unroll=True)

        def add_chunk(self, q):
            self.po[q] = (self.po[q].astype(F32) + self.r1[q].astype(F32)).astype(BF)

        def spread(self, kind, i):
            for q in range(2):
                to = flip(zl, i) * 2 + q
                src = self.po.at[to * 2 + (1 - zh if kind == 0 else zh)]

                @pl.when(to != y)
                def _():
                    rc(src, self.r2.at[kind, y], self.left, self.base + 4 + kind, (node_of(to, zh, c), l)).start()

        def arrive(self, kind):
            view = self.r2.at[kind, pl.ds(0, 7)]
            rc(view, view, self.left, self.base + 4 + kind, sib).wait_recv()

        def total(self, kind):
            def add(j, acc):
                return acc + self.r2[kind, (y - peer(j) + 8) % 8].astype(F32)

            return lax.fori_loop(0, 7, add, self.po[y * 2 + (1 - zh if kind == 0 else zh)].astype(F32), unroll=True)

        def cross(self):
            self.arrive(0)
            self.t3[...] = self.total(0).astype(BF)
            go((self, "zh"), 1, lambda j: rc(self.t3, self.r3, self.left, self.base + 6, zhp))

        def finish(self):
            mine = self.total(1)
            got((self, "zh"))
            return mine + self.r3[...].astype(F32)

    def factor_of(sums):
        return lax.rsqrt(jnp.sum(sums, axis=1, keepdims=True) / 4096.0 + EPS)

    def rms_factor(buf):
        def add(j, acc):
            v = buf[j, 0:128, :].astype(F32)
            return acc + v * v

        sums = lax.fori_loop(0, 32, add, jnp.zeros((128, 128), F32), unroll=4)
        fac[...] = jnp.broadcast_to(factor_of(sums), (128, 128))

    def gain_row(j):
        return x0[j, 128:144, :].astype(F32)[0:1, :]

    def normalize(buf):
        rms_factor(buf)

        def one(q):
            for h in range(2):
                j = q * 2 + h
                v = buf[j, 0:128, :].astype(F32) * fac[...] * gain_row(j)
                nb[q, :, h * 128:(h + 1) * 128] = v.astype(BF)

        loop(16, one, unroll=4)

    def up_chunk(q):
        pre[...] += lax.dot_general(nb[q], up[q], NT, preferred_element_type=F32)

    def pre_item(i):
        loop(4, lambda q: up_chunk(flip(zl, i) * 4 + q), unroll=True)

    def raw_chunk(q):
        halves = []
        for h in range(2):
            v = x1[q * 2 + h].astype(F32)
            fac[...] += v * v
            halves.append((v * gain_row(q * 2 + h)).astype(BF))
        pre[...] += lax.dot_general(jnp.concatenate(halves, axis=1), up[q], NT, preferred_element_type=F32)

    def slope_chunk(q):
        rows = jnp.concatenate([cot[q * 2], cot[q * 2 + 1]], axis=1)
        slope[...] += lax.dot_general(rows, dn[q], NT, preferred_element_type=F32)

    def activate(transposed):
        v = pre[...]
        h = v * jax.nn.sigmoid(v)
        hid[...] = h.astype(BF)
        hf[:, 0:448] = h
        for b in range(4):
            rows = 128 if b < 3 else 64
            block = hf[:, b * 128:(b + 1) * 128].T
            transposed[l, b * 128:b * 128 + rows, :] = block[0:rows, :].astype(BF)

    def out_chunk(left, weight, q, red):
        res = lax.dot_general(left, weight[q], NN, preferred_element_type=F32).astype(BF)
        low, high = res[:, 0:128], res[:, 128:256]
        even = c == 0
        red.po[q, 0:128, :] = jnp.where(even, low, high)
        red.ps[q, 0:128, :] = jnp.where(even, high, low)

    def out_item(left, weight, i, red):
        loop(4, lambda q: out_chunk(left[...], weight, flip(zl, i) * 4 + q, red), unroll=True)
        red.send(i)

    ag_a, ag_b, sg_a, lg_a, lg_b = (recvs.take(k) for k in (31, 31, 28, 15, 15))
    ag_x0, ag_cot, ag_x1 = NodeGather(x0, ag_a), NodeGather(cot, ag_b), NodeGather(x1, ag_a)
    sg_cot, sg_g1 = SeededGather(cott, sg_a), SeededGather(g1t, sg_a)
    lg_up, lg_dn = LocalGather(up, lg_a), LocalGather(dn, lg_b)
    lg_h1, lg_h2 = LocalGather(h1t, lg_a), LocalGather(h2t, lg_b)
    rs_1 = NodeReduce(po1, ps1, r11, r21, r31, t31)
    rs_g = NodeReduce(pog, psg, r1g, r2g, r3g, t3g)
    rs_2 = NodeReduce(po2, ps2, r12, r22, r32, t32)
    assert sends.used <= N_SEND and recvs.used <= N_RECV, (sends.used, recvs.used)

    barrier = pltpu.get_barrier_semaphore()

    def greet(dev):
        pl.semaphore_signal(barrier, inc=1, device_id=dev, device_id_type=MESH)

    for k in range(4):
        source = node_of((y + 4 * (k // 2)) % 8, (zh + k % 2) % 2, c) // 2
        if k == 0:
            @pl.when(moved)
            def _():
                greet((l * 2 + c, source))
        else:
            greet((l * 2 + c, source))

    greet(zhp)
    loop(7, lambda j: greet(ydev(peer(j))))
    for i in range(1, 4):
        greet(zdev(i))
    greet(xdev(1))
    greet(xdev(-1))
    greet(sib)

    x0[n, 0:128, :] = tok_in[...]
    x0[n, 128:144, :] = jnp.broadcast_to(gain_in[...].astype(F32), (16, 128)).astype(BF)
    for q_in, s_in, weight in ((up_q, up_s, up), (dn_q, dn_s, dn)):
        for a in range(2):
            cols = pl.ds(a * 128, 128)
            for b in range(4):
                size = 128 if b < 3 else 64
                rows = pl.ds(b * 128, size)
                hf[0:128, 0:size] = jnp.broadcast_to(s_in[a:a + 1, rows].astype(F32), (128, size))
                scale = hf[:, 0:128].T[0:size, :]
                weight[l, rows, cols] = (q_in[rows, cols].astype(F32) * scale).astype(BF)
    hf[...] = jnp.zeros_like(hf)
    cot[n] = cot_in[...]
    pre[...] = jnp.zeros_like(pre)
    slope[...] = jnp.zeros_like(slope)

    @pl.when(moved)
    def _():
        pl.semaphore_wait(barrier, 18)

    @pl.when(jnp.logical_not(moved))
    def _():
        pl.semaphore_wait(barrier, 17)

    lg_up.z(1)
    lg_up.full(0)
    ag_x0.start()
    lg_up.z(2)
    lg_dn.full(0)
    sg_cot.scatter(cot_in)
    ag_x0.mid()
    lg_up.relay(0)
    lg_up.wait_z(1)
    lg_up.full(1)
    lg_up.z(3)
    lg_dn.relay(0)
    lg_up.wait_z(2)
    lg_up.full(2)
    lg_dn.z(1)
    ag_x0.end()
    ag_cot.start()
    normalize(x0)
    lg_up.done(0)
    pre_item(0)
    lg_up.relay(1)
    lg_up.wait_z(3)
    lg_up.full(3)
    lg_dn.z(2)
    lg_up.relay(2)
    ag_cot.mid()
    lg_dn.wait_z(1)
    lg_dn.full(1)
    lg_dn.z(3)
    lg_up.done(1)
    pre_item(1)
    lg_up.relay(3)
    lg_dn.wait_z(2)
    lg_dn.full(2)
    lg_up.done(2)
    pre_item(2)
    lg_dn.relay(1)
    lg_dn.wait_z(3)
    lg_dn.full(3)
    lg_up.done(3)
    pre_item(3)
    activate(h1t)
    lg_dn.done(0)
    out_item(hid, dn, 0, rs_1)
    sg_cot.seeded(cot_in)
    sg_cot.spread()
    lg_dn.relay(2)
    ag_cot.end()
    rs_1.combine(0)
    rs_1.spread(0, 0)
    rs_1.spread(1, 0)
    lg_dn.done(1)
    out_item(hid, dn, 1, rs_1)
    lg_dn.relay(3)
    rs_1.combine(1)
    rs_1.spread(0, 1)
    rs_1.spread(1, 1)
    lg_dn.done(2)
    out_item(hid, dn, 2, rs_1)
    rs_1.combine(2)
    rs_1.spread(0, 2)
    rs_1.spread(1, 2)
    lg_dn.done(3)
    out_item(hid, dn, 3, rs_1)
    rs_1.combine(3)
    rs_1.spread(0, 3)
    rs_1.spread(1, 3)
    loop(16, slope_chunk, unroll=4)
    rs_1.cross()
    rs_1.arrive(1)
    x1[n] = (x0[n, 0:128, :].astype(F32) + rs_1.finish()).astype(BF)

    ag_x1.start()
    pre[...] = jnp.zeros_like(pre)
    fac[...] = jnp.zeros_like(fac)
    sg_cot.end(lambda q: None)
    ag_x1.mid()
    for i in range(1, 4):
        lg_h1.z(i)
    lg_h1.full(0)
    ag_x1.end(raw_chunk)
    factor = factor_of(fac[...])
    fac[...] = jnp.broadcast_to(factor, (128, 128))
    pre[...] = pre[...] * factor
    activate(h2t)
    for i in range(1, 4):
        lg_h1.wait_z(i)
        lg_h1.full(i)
    for i in range(1, 4):
        lg_h2.z(i)

    v = pre[...]
    sig = jax.nn.sigmoid(v)
    grad_pre = (slope[...] * (sig * (1.0 + v * (1.0 - sig)))).astype(BF)
    pulled = jnp.sum(grad_pre.astype(F32) * v, axis=1, keepdims=True)
    pulled = jnp.broadcast_to(pulled, (128, 128)).T[0:16, :].astype(BF)

    def put(j):
        pog[j, 128:144, :] = pulled
        psg[j, 128:144, :] = pulled

    loop(16, put)
    for i in range(4):
        loop(4, lambda q: out_chunk(grad_pre, up, flip(zl, i) * 4 + q, rs_g), unroll=True)
        rs_g.send(i)
        if i > 0:
            rs_g.combine(i - 1)
            rs_g.spread(0, i - 1)
    rs_g.combine(3)
    rs_g.spread(0, 3)
    for i in range(4):
        rs_g.spread(1, i)
    for i in range(4):
        out_item(hid, dn, i, rs_2)
    for i in range(4):
        rs_2.combine(i)
    rs_g.cross()
    for i in range(4):
        lg_h1.relay(i)
    lg_h2.full(0)
    for i in range(1, 4):
        lg_h2.wait_z(i)
        lg_h2.full(i)
    rs_g.arrive(1)
    tot[...] = rs_g.finish()
    inner = jnp.broadcast_to(tot[128:129, :], (128, 128)).T / 4096.0
    x1_own = x1[n].astype(F32)
    scaled = tot[0:128, :] * gain_row(n)
    factor = fac[...]
    gp[...] = (cot[n].astype(F32) + factor * scaled - x1_own * factor * factor * inner).astype(BF)
    sg_g1.scatter(gp)
    for i in range(4):
        rs_2.spread(0, i)
    for i in range(4):
        rs_2.spread(1, i)
    for i in range(4):
        lg_h1.done(i)
        lg_h2.relay(i)
    gacc[...] = jnp.zeros_like(gacc)
    sg_g1.seeded(gp)
    sg_g1.spread()

    def grad_chunk(hidden, grads):
        def one(q):
            right = jnp.concatenate([grads[q * 2], grads[q * 2 + 1]], axis=1)
            gacc[...] += lax.dot_general(hidden[q], right, NN, preferred_element_type=F32)
        return one

    for i in range(4):
        lg_h2.done(i)
        loop(4, lambda q: grad_chunk(h2t, cott)(flip(zl, i) * 4 + q), unroll=True)
    last = grad_chunk(h1t, g1t)
    sg_g1.end(last, rs_2.cross)
    rs_2.arrive(1)
    states_out[...] = (x1_own + rs_2.finish()).astype(BF)
    grad_out[...] = gacc[...].astype(BF)
    sg_cot.scattered(cot_in)
    sg_g1.scattered(gp)
    drain()


def per_device(tokens, cotangent, gain, up_q, up_scale, down_q, down_scale):
    vmem = pl.BlockSpec(memory_space=pltpu.VMEM)

    def reduce_scratch(rows):
        wide = pltpu.VMEM((16, rows, 128), BF)
        one = pltpu.VMEM((rows, 128), BF)
        return [wide, wide, wide, pltpu.VMEM((2, 8, rows, 128), BF), one, one]

    full = pltpu.VMEM((16, 448, 256), BF)
    act = pltpu.VMEM((32, 128, 128), BF)
    hidden_all = pltpu.VMEM((16, 448, 128), BF)
    scratch = [
        full, full, pltpu.VMEM((32, 144, 128), BF), act, act, act, act,
        pltpu.VMEM((16, 128, 256), BF), hidden_all, hidden_all,
        pltpu.VMEM((128, 448), BF), pltpu.VMEM((128, 512), F32),
        pltpu.VMEM((128, 448), F32), pltpu.VMEM((128, 448), F32),
        pltpu.VMEM((448, 256), F32), pltpu.VMEM((128, 128), F32),
        pltpu.VMEM((128, 128), BF), pltpu.VMEM((144, 128), F32),
    ]
    scratch += reduce_scratch(128) + reduce_scratch(144) + reduce_scratch(128)
    scratch += [pltpu.SemaphoreType.DMA((N_SEND,)), pltpu.SemaphoreType.DMA((N_RECV,))]
    return pl.pallas_call(
        kernel,
        out_shape=(
            jax.ShapeDtypeStruct((128, 128), BF),
            jax.ShapeDtypeStruct((448, 256), BF),
        ),
        in_specs=[vmem] * 7,
        out_specs=(vmem, vmem),
        scratch_shapes=scratch,
        compiler_params=pltpu.CompilerParams(
            collective_id=0, has_side_effects=True, vmem_limit_bytes=48 << 20
        ),
        name="looped_block",
    )(tokens, cotangent, gain, up_q.T, up_scale, down_q, down_scale.T)


def solution(mesh):
    in_specs = (
        P("local", "node"),
        P("local", "node"),
        P(None, "node"),
        P("local", "node"),
        P("local", "node"),
        P("node", "local"),
        P("node", "local"),
    )
    out_specs = (P("local", "node"), P("node", "local"))
    return jax.shard_map(
        per_device, mesh=mesh, in_specs=in_specs, out_specs=out_specs, check_vma=False
    )
```

```python
import jax
import jax.numpy as jnp
from jax import lax
from jax.experimental import pallas as pl
from jax.experimental.pallas import tpu as pltpu
from jax.sharding import PartitionSpec as P

MESH = pl.DeviceIdType.MESH
BF = jnp.bfloat16
F32 = jnp.float32
EPS = 1e-05
NT = (((1,), (1,)), ((), ()))
NN = (((1,), (0,)), ((), ()))


def peer(j):
    far = j // 2 + 1
    return far + (j % 2) * (8 - 2 * far)


def flip(a, i):
    return ((a // 2 + i // 2) % 2) * 2 + (a % 2 + i % 2) % 2


class Sems:
    def __init__(self):
        self.used = 0

    def take(self, count):
        base = self.used
        self.used += count
        return base


N_SEND = 24
N_RECV = 152


def kernel(
    tok_in, cot_in, gain_in, up_q, up_s, dn_q, dn_s, states_out, grad_out,
    up, dn, x0, x1, cot, cott, g1t, nb, h1t, h2t, hid, hf, pre, slope, gacc, fac, gp, tot,
    po1, ps1, r11, r21, r31, t31,
    pog, psg, r1g, r2g, r3g, t3g,
    po2, ps2, r12, r22, r32, t32,
    ss, rs,
):
    n = lax.axis_index("node")
    l = lax.axis_index("local")
    y, zh, c = n // 4, (n // 2) % 2, n % 2
    zl, x = l // 4, l % 4
    sends, recvs = Sems(), Sems()

    def node_of(y_, zh_, c_):
        return (y_ * 2 + zh_) * 2 + c_

    sib = (node_of(y, zh, 1 - c), l)
    zhp = (node_of(y, 1 - zh, c), l)
    own_m = node_of(y, 1 - zh, c)

    def ydev(k):
        return (node_of((y + k) % 8, zh, c), l)

    def xdev(d):
        return (n, zl * 4 + (x + d + 4) % 4)

    def zdev(i):
        return (n, flip(zl, i) * 4 + x)

    moved = n // 2 != l

    def rc(src, dst, send, recv, dev):
        return pltpu.make_async_remote_copy(
            src_ref=src, dst_ref=dst, send_sem=ss.at[send], recv_sem=rs.at[recv],
            device_id=dev, device_id_type=MESH,
        )

    def loop(count, body, first=0, unroll=1):
        if count - first == 1:
            body(first)
            return

        def step(j, carry):
            body(j)
            return carry

        lax.fori_loop(first, count, step, 0, unroll=unroll)

    pending = {}
    departures = []

    def go(key, count, copy):
        assert key not in pending
        pending[key] = count, copy
        loop(count, lambda j: copy(j).start())

    def got(key):
        count, copy = pending.pop(key)
        loop(count, lambda j: copy(j).wait_recv())

    def departing(view):
        sem = sends.take(1)
        departures.append((view, sem))
        return sem

    def drain():
        assert not pending
        for view, sem in departures:
            rc(view, view, sem, 0, sib).wait_send()

    class NodeGather:
        def __init__(self, buf, base):
            self.buf, self.base = buf, base
            self.left = departing(buf.at[pl.ds(0, 31)])

        def copy(self, slot, sem, dev):
            return rc(self.buf.at[slot], self.buf.at[slot], self.left, self.base + sem, dev)

        def from_y(self, j, zh_):
            return node_of((y - peer(j) + 8) % 8, zh_, c)

        def first(self):
            go((self, "zh"), 1, lambda j: self.copy(n, 1, zhp))
            go((self, "sib"), 1, lambda j: self.copy(n, 0, sib))

        def start(self):
            go((self, "own"), 7, lambda j: self.copy(n, 2 + j, ydev(peer(j))))

        def mid(self):
            got((self, "zh"))
            go((self, "other"), 7, lambda j: self.copy(own_m, 9 + j, ydev(peer(j))))
            go((self, "sib_zh"), 1, lambda j: self.copy(own_m, 16, sib))

        def pass_on(self, key, zh_, sem, use):
            count, came = pending.pop((self, key))

            def copy(j):
                return self.copy(self.from_y(j, zh_), sem + j, sib)

            def move(j):
                came(j).wait_recv()
                copy(j).start()

            def finish(j):
                copy(j).wait_recv()
                use(((y - peer(j) + 8) % 8) * 2 + zh_)

            def both(j):
                move(j)
                finish(j - 1)

            move(0)
            loop(count, both, first=1)
            finish(count - 1)

        def end(self, use=lambda q: None):
            got((self, "sib"))
            use(y * 2 + zh)
            got((self, "sib_zh"))
            use(y * 2 + 1 - zh)
            self.pass_on("own", zh, 17, use)
            self.pass_on("other", 1 - zh, 24, use)

    class SeededGather:
        def __init__(self, buf, base):
            self.buf, self.base, self.perm = buf, base, recvs.take(4)
            self.left = departing(buf.at[pl.ds(0, 28)])
            self.perm_left = sends.take(4)

        def seed(self, k):
            return node_of((y + 4 * (k // 2)) % 8, (zh + k % 2) % 2, c)

        def scatter_copy(self, src, k):
            to = node_of((l // 2 + 4 * (k // 2)) % 8, (l % 2 + k % 2) % 2, c)
            return rc(src, self.buf.at[l * 2 + c], self.perm_left + k, self.perm + k, (to, n // 2))

        def scatter(self, src):
            @pl.when(moved)
            def _():
                self.scatter_copy(src, 0).start()

            @pl.when(jnp.logical_not(moved))
            def _():
                self.buf[l * 2 + c] = src[...]

            for k in range(1, 4):
                self.scatter_copy(src, k).start()

        def seeded(self, src):
            @pl.when(moved)
            def _():
                self.scatter_copy(src, 0).wait_recv()

            for k in range(1, 4):
                self.scatter_copy(src, k).wait_recv()

        def scattered(self, src):
            @pl.when(moved)
            def _():
                self.scatter_copy(src, 0).wait_send()

            for k in range(1, 4):
                self.scatter_copy(src, k).wait_send()

        def copy(self, slot, sem, dev):
            return rc(self.buf.at[slot], self.buf.at[slot], self.left, self.base + sem, dev)

        def step(self, r, k):
            return (1, 7)[r] if r < 2 else 2 + 4 * (k % 2)

        def spread(self):
            for r in range(3):
                loop(4, lambda k: self.copy(self.seed(k), r * 4 + k, ydev(self.step(r, k))).start())
            loop(4, lambda k: self.copy(self.seed(k), 12 + k, sib).start())

        def arrival(self, r, k):
            from_y = (y - self.step(r, k) + 8) % 8
            return node_of((from_y + 4 * (k // 2)) % 8, (zh + k % 2) % 2, c)

        def end(self, use, between=lambda: None):
            def move(r, k):
                slot = self.arrival(r, k)
                self.copy(slot, r * 4 + k, sib).wait_recv()
                self.copy(slot, 16 + r * 4 + k, sib).start()

            def finish(r, k):
                slot = self.arrival(r, k)
                self.copy(slot, 16 + r * 4 + k, sib).wait_recv()
                use(slot // 2)

            def seeds(k):
                self.copy(self.seed(k), 12 + k, sib).wait_recv()
                use(self.seed(k) // 2)

            loop(4, seeds)
            for r in range(3):
                if r == 2:
                    between()
                loop(4, lambda k: move(r, k))
                if r > 0:
                    loop(4, lambda k: finish(r - 1, k))
            loop(4, lambda k: finish(2, k))

    class LocalGather:
        def __init__(self, buf, base):
            self.buf, self.base = buf, base
            self.half = buf.shape[1] // 2
            self.left = departing(buf.at[pl.ds(0, 15)])

        def slot(self, i, d):
            return flip(zl, i) * 4 + (x + d + 4) % 4

        def z(self, i):
            go((self, "z", i), 1, lambda j: rc(self.buf.at[l], self.buf.at[l], self.left, self.base + i - 1, zdev(i)))

        def wait_z(self, i):
            got((self, "z", i))

        def full(self, i):
            s = self.buf.at[self.slot(i, 0)]
            for d in (1, -1):
                go((self, "x", i, d), 1, lambda j, d=d: rc(s, s, self.left, self.base + 3 + 2 * i + (d < 0), xdev(d)))

        def relay(self, i):
            for d in (1, -1):
                ref = self.buf.at[self.slot(i, -d), pl.ds(0 if d > 0 else self.half, self.half)]
                got((self, "x", i, d))
                rc(ref, ref, self.left, self.base + 11 + i, xdev(d)).start()

        def done(self, i):
            s = self.buf.at[self.slot(i, 2)]
            rc(s, s, self.left, self.base + 11 + i, xdev(1)).wait_recv()

    class NodeReduce:
        def __init__(self, po, ps, r1, r2, r3, t3):
            self.po, self.ps, self.r1, self.r2, self.r3, self.t3 = po, ps, r1, r2, r3, t3
            self.base = recvs.take(7)
            self.sib_left = departing(ps)
            self.left = departing(po.at[pl.ds(0, 15)])

        def send(self, i):
            rows = pl.ds(flip(zl, i) * 4, 4)
            go((self, "sib", i), 1, lambda j: rc(self.ps.at[rows], self.r1.at[rows], self.sib_left, self.base + i, sib))

        def combine(self, i):
            got((self, "sib", i))
            loop(4, lambda q: self.add_chunk(flip(zl, i) * 4 + q), unroll=True)

        def add_chunk(self, q):
            self.po[q] = (self.po[q].astype(F32) + self.r1[q].astype(F32)).astype(BF)

        def spread(self, kind, i):
            for q in range(2):
                to = flip(zl, i) * 2 + q
                src = self.po.at[to * 2 + (1 - zh if kind == 0 else zh)]

                @pl.when(to != y)
                def _():
                    rc(src, self.r2.at[kind, y], self.left, self.base + 4 + kind, (node_of(to, zh, c), l)).start()

        def spread_all(self, kind):
            def one(j):
                to = (y + peer(j)) % 8
                src = self.po.at[to * 2 + (1 - zh if kind == 0 else zh)]
                rc(src, self.r2.at[kind, y], self.left, self.base + 4 + kind, ydev(peer(j))).start()

            loop(7, one)

        def arrive(self, kind):
            view = self.r2.at[kind, pl.ds(0, 7)]
            rc(view, view, self.left, self.base + 4 + kind, sib).wait_recv()

        def total(self, kind):
            def add(j, acc):
                return acc + self.r2[kind, (y - peer(j) + 8) % 8].astype(F32)

            return lax.fori_loop(0, 7, add, self.po[y * 2 + (1 - zh if kind == 0 else zh)].astype(F32), unroll=True)

        def cross(self):
            self.arrive(0)
            self.t3[...] = self.total(0).astype(BF)
            go((self, "zh"), 1, lambda j: rc(self.t3, self.r3, self.left, self.base + 6, zhp))

        def finish(self):
            mine = self.total(1)
            got((self, "zh"))
            return mine + self.r3[...].astype(F32)

    def factor_of(sums):
        return lax.rsqrt(jnp.sum(sums, axis=1, keepdims=True) / 4096.0 + EPS)

    def rms_factor(buf):
        def add(j, acc):
            v = buf[j, 0:128, :].astype(F32)
            return acc + v * v

        sums = lax.fori_loop(0, 32, add, jnp.zeros((128, 128), F32), unroll=4)
        fac[...] = jnp.broadcast_to(factor_of(sums), (128, 128))

    def gain_row(j):
        return x0[j, 128:144, :].astype(F32)[0:1, :]

    def normalize(buf):
        rms_factor(buf)

        def one(q):
            for h in range(2):
                j = q * 2 + h
                v = buf[j, 0:128, :].astype(F32) * fac[...] * gain_row(j)
                nb[q, :, h * 128:(h + 1) * 128] = v.astype(BF)

        loop(16, one, unroll=4)

    def up_chunk(q):
        pre[...] += lax.dot_general(nb[q], up[q], NT, preferred_element_type=F32)

    def pre_item(i):
        loop(4, lambda q: up_chunk(flip(zl, i) * 4 + q), unroll=True)

    def raw_chunk(q):
        halves = []
        for h in range(2):
            v = x1[q * 2 + h].astype(F32)
            fac[...] += v * v
            halves.append((v * gain_row(q * 2 + h)).astype(BF))
        pre[...] += lax.dot_general(jnp.concatenate(halves, axis=1), up[q], NT, preferred_element_type=F32)

    def slope_chunk(q):
        rows = jnp.concatenate([cot[q * 2], cot[q * 2 + 1]], axis=1)
        slope[...] += lax.dot_general(rows, dn[q], NT, preferred_element_type=F32)

    def activate(transposed):
        v = pre[...]
        h = v * jax.nn.sigmoid(v)
        hid[...] = h.astype(BF)
        hf[:, 0:448] = h
        for b in range(4):
            rows = 128 if b < 3 else 64
            block = hf[:, b * 128:(b + 1) * 128].T
            transposed[l, b * 128:b * 128 + rows, :] = block[0:rows, :].astype(BF)

    def out_chunk(left, weight, q, red):
        res = lax.dot_general(left, weight[q], NN, preferred_element_type=F32).astype(BF)
        low, high = res[:, 0:128], res[:, 128:256]
        even = c == 0
        red.po[q, 0:128, :] = jnp.where(even, low, high)
        red.ps[q, 0:128, :] = jnp.where(even, high, low)

    def out_item(left, weight, i, red):
        loop(4, lambda q: out_chunk(left[...], weight, flip(zl, i) * 4 + q, red), unroll=True)
        red.send(i)

    ag_a, ag_b, sg_a, lg_a, lg_b = (recvs.take(k) for k in (31, 31, 28, 15, 15))
    ag_x0, ag_cot, ag_x1 = NodeGather(x0, ag_a), NodeGather(cot, ag_b), NodeGather(x1, ag_a)
    sg_cot, sg_g1 = SeededGather(cott, sg_a), SeededGather(g1t, sg_a)
    lg_up, lg_dn = LocalGather(up, lg_a), LocalGather(dn, lg_b)
    lg_h1, lg_h2 = LocalGather(h1t, lg_a), LocalGather(h2t, lg_b)
    rs_1 = NodeReduce(po1, ps1, r11, r21, r31, t31)
    rs_g = NodeReduce(pog, psg, r1g, r2g, r3g, t3g)
    rs_2 = NodeReduce(po2, ps2, r12, r22, r32, t32)
    assert sends.used <= N_SEND and recvs.used <= N_RECV, (sends.used, recvs.used)

    barrier = pltpu.get_barrier_semaphore()

    def greet(dev):
        pl.semaphore_signal(barrier, inc=1, device_id=dev, device_id_type=MESH)

    for k in range(4):
        source = node_of((y + 4 * (k // 2)) % 8, (zh + k % 2) % 2, c) // 2
        if k == 0:
            @pl.when(moved)
            def _():
                greet((l * 2 + c, source))
        else:
            greet((l * 2 + c, source))

    greet(zhp)
    loop(7, lambda j: greet(ydev(peer(j))))
    for i in range(1, 4):
        greet(zdev(i))
    greet(xdev(1))
    greet(xdev(-1))
    greet(sib)

    x0[n, 0:128, :] = tok_in[...]
    x0[n, 128:144, :] = jnp.broadcast_to(gain_in[...].astype(F32), (16, 128)).astype(BF)
    for q_in, s_in, weight in ((up_q, up_s, up), (dn_q, dn_s, dn)):
        for a in range(2):
            cols = pl.ds(a * 128, 128)
            for b in range(4):
                size = 128 if b < 3 else 64
                rows = pl.ds(b * 128, size)
                hf[0:128, 0:size] = jnp.broadcast_to(s_in[a:a + 1, rows].astype(F32), (128, size))
                scale = hf[:, 0:128].T[0:size, :]
                weight[l, rows, cols] = (q_in[rows, cols].astype(F32) * scale).astype(BF)
    hf[...] = jnp.zeros_like(hf)
    cot[n] = cot_in[...]
    pre[...] = jnp.zeros_like(pre)
    slope[...] = jnp.zeros_like(slope)

    @pl.when(moved)
    def _():
        pl.semaphore_wait(barrier, 18)

    @pl.when(jnp.logical_not(moved))
    def _():
        pl.semaphore_wait(barrier, 17)

    ag_x0.first()
    ag_cot.first()
    lg_up.z(1)
    lg_up.full(0)
    ag_x0.start()
    lg_up.z(2)
    lg_dn.full(0)
    sg_cot.scatter(cot_in)
    ag_x0.mid()
    lg_up.relay(0)
    lg_up.wait_z(1)
    lg_up.full(1)
    lg_up.z(3)
    lg_dn.relay(0)
    lg_up.wait_z(2)
    lg_up.full(2)
    lg_dn.z(1)
    ag_x0.end()
    ag_cot.start()
    normalize(x0)
    ag_cot.mid()
    lg_up.done(0)
    pre_item(0)
    lg_up.relay(1)
    lg_up.wait_z(3)
    lg_up.full(3)
    lg_dn.z(2)
    lg_up.relay(2)
    lg_dn.wait_z(1)
    lg_dn.full(1)
    lg_dn.z(3)
    lg_up.done(1)
    pre_item(1)
    lg_up.relay(3)
    lg_dn.wait_z(2)
    lg_dn.full(2)
    lg_up.done(2)
    pre_item(2)
    lg_dn.relay(1)
    lg_dn.wait_z(3)
    lg_dn.full(3)
    lg_up.done(3)
    pre_item(3)
    activate(h1t)
    lg_dn.done(0)
    out_item(hid, dn, 0, rs_1)
    sg_cot.seeded(cot_in)
    sg_cot.spread()
    lg_dn.relay(2)
    ag_cot.end()
    rs_1.combine(0)
    rs_1.spread(0, 0)
    rs_1.spread(1, 0)
    lg_dn.done(1)
    out_item(hid, dn, 1, rs_1)
    lg_dn.relay(3)
    rs_1.combine(1)
    rs_1.spread(0, 1)
    rs_1.spread(1, 1)
    lg_dn.done(2)
    out_item(hid, dn, 2, rs_1)
    rs_1.combine(2)
    rs_1.spread(0, 2)
    rs_1.spread(1, 2)
    lg_dn.done(3)
    out_item(hid, dn, 3, rs_1)
    rs_1.combine(3)
    rs_1.spread(0, 3)
    rs_1.spread(1, 3)
    loop(16, slope_chunk, unroll=4)
    rs_1.cross()
    rs_1.arrive(1)
    x1[n] = (x0[n, 0:128, :].astype(F32) + rs_1.finish()).astype(BF)

    ag_x1.first()
    ag_x1.start()
    pre[...] = jnp.zeros_like(pre)
    fac[...] = jnp.zeros_like(fac)
    sg_cot.end(lambda q: None)
    ag_x1.mid()
    for i in range(1, 4):
        lg_h1.z(i)
    lg_h1.full(0)
    ag_x1.end(raw_chunk)
    factor = factor_of(fac[...])
    fac[...] = jnp.broadcast_to(factor, (128, 128))
    pre[...] = pre[...] * factor
    activate(h2t)
    for i in range(1, 4):
        lg_h1.wait_z(i)
        lg_h1.full(i)
    for i in range(1, 4):
        lg_h2.z(i)

    v = pre[...]
    sig = jax.nn.sigmoid(v)
    grad_pre = (slope[...] * (sig * (1.0 + v * (1.0 - sig)))).astype(BF)
    pulled = jnp.sum(grad_pre.astype(F32) * v, axis=1, keepdims=True)
    pulled = jnp.broadcast_to(pulled, (128, 128)).T[0:16, :].astype(BF)

    def put(j):
        pog[j, 128:144, :] = pulled
        psg[j, 128:144, :] = pulled

    loop(16, put)
    for i in range(4):
        loop(4, lambda q: out_chunk(grad_pre, up, flip(zl, i) * 4 + q, rs_g), unroll=True)
        rs_g.send(i)
        if i > 0:
            rs_g.combine(i - 1)
    rs_g.combine(3)
    rs_g.spread_all(0)
    rs_g.spread_all(1)
    for i in range(4):
        out_item(hid, dn, i, rs_2)
    for i in range(4):
        rs_2.combine(i)
    rs_g.cross()
    for i in range(4):
        lg_h1.relay(i)
    lg_h2.full(0)
    for i in range(1, 4):
        lg_h2.wait_z(i)
        lg_h2.full(i)
    rs_g.arrive(1)
    tot[...] = rs_g.finish()
    inner = jnp.broadcast_to(tot[128:129, :], (128, 128)).T / 4096.0
    x1_own = x1[n].astype(F32)
    scaled = tot[0:128, :] * gain_row(n)
    factor = fac[...]
    gp[...] = (cot[n].astype(F32) + factor * scaled - x1_own * factor * factor * inner).astype(BF)
    sg_g1.scatter(gp)
    rs_2.spread_all(0)
    rs_2.spread_all(1)
    for i in range(4):
        lg_h1.done(i)
        lg_h2.relay(i)
    gacc[...] = jnp.zeros_like(gacc)
    sg_g1.seeded(gp)
    sg_g1.spread()

    def grad_chunk(hidden, grads):
        def one(q):
            right = jnp.concatenate([grads[q * 2], grads[q * 2 + 1]], axis=1)
            gacc[...] += lax.dot_general(hidden[q], right, NN, preferred_element_type=F32)
        return one

    for i in range(4):
        lg_h2.done(i)
        loop(4, lambda q: grad_chunk(h2t, cott)(flip(zl, i) * 4 + q), unroll=True)
    last = grad_chunk(h1t, g1t)
    sg_g1.end(last, rs_2.cross)
    rs_2.arrive(1)
    states_out[...] = (x1_own + rs_2.finish()).astype(BF)
    grad_out[...] = gacc[...].astype(BF)
    sg_cot.scattered(cot_in)
    sg_g1.scattered(gp)
    drain()


def per_device(tokens, cotangent, gain, up_q, up_scale, down_q, down_scale):
    vmem = pl.BlockSpec(memory_space=pltpu.VMEM)

    def reduce_scratch(rows):
        wide = pltpu.VMEM((16, rows, 128), BF)
        one = pltpu.VMEM((rows, 128), BF)
        return [wide, wide, wide, pltpu.VMEM((2, 8, rows, 128), BF), one, one]

    full = pltpu.VMEM((16, 448, 256), BF)
    act = pltpu.VMEM((32, 128, 128), BF)
    hidden_all = pltpu.VMEM((16, 448, 128), BF)
    scratch = [
        full, full, pltpu.VMEM((32, 144, 128), BF), act, act, act, act,
        pltpu.VMEM((16, 128, 256), BF), hidden_all, hidden_all,
        pltpu.VMEM((128, 448), BF), pltpu.VMEM((128, 512), F32),
        pltpu.VMEM((128, 448), F32), pltpu.VMEM((128, 448), F32),
        pltpu.VMEM((448, 256), F32), pltpu.VMEM((128, 128), F32),
        pltpu.VMEM((128, 128), BF), pltpu.VMEM((144, 128), F32),
    ]
    scratch += reduce_scratch(128) + reduce_scratch(144) + reduce_scratch(128)
    scratch += [pltpu.SemaphoreType.DMA((N_SEND,)), pltpu.SemaphoreType.DMA((N_RECV,))]
    return pl.pallas_call(
        kernel,
        out_shape=(
            jax.ShapeDtypeStruct((128, 128), BF),
            jax.ShapeDtypeStruct((448, 256), BF),
        ),
        in_specs=[vmem] * 7,
        out_specs=(vmem, vmem),
        scratch_shapes=scratch,
        compiler_params=pltpu.CompilerParams(
            collective_id=0, has_side_effects=True, vmem_limit_bytes=48 << 20
        ),
        name="looped_block",
    )(tokens, cotangent, gain, up_q.T, up_scale, down_q, down_scale.T)


def solution(mesh):
    in_specs = (
        P("local", "node"),
        P("local", "node"),
        P(None, "node"),
        P("local", "node"),
        P("local", "node"),
        P("node", "local"),
        P("node", "local"),
    )
    out_specs = (P("local", "node"), P("node", "local"))
    return jax.shard_map(
        per_device, mesh=mesh, in_specs=in_specs, out_specs=out_specs, check_vma=False
    )
```
